512 devices in a mesh: seq: 64 (over y_lo, x, z), head: 8 (over y_hi, core).
Axes of the slice: x: 4, y: 8 (y_hi: 4, y_lo: 2; y = y_hi * 2 + y_lo), z: 8, core: 2. Of those that a mesh axis runs over, the one named last changes fastest.
Arguments:
- queries: bfloat16 [49152, 2048], P(('seq', 'head')), may hold values from -6 to 6
- keys: bfloat16 [49152, 2048], P(('seq', 'head')), may hold values from -6 to 6
- values: bfloat16 [49152, 2048], P(('seq', 'head')), may hold values from -6 to 6
- out_grad: bfloat16 [49152, 2048], P(('seq', 'head')), may hold values from -6 to 6
- window: int32 [16, 2], replicated, may hold values from 0 to 1, as said below
Outputs:
- grad_queries: bfloat16 [49152, 2048], P(('seq', 'head'))
- grad_keys: bfloat16 [49152, 2048], P(('seq', 'head'))
- grad_values: bfloat16 [49152, 2048], P(('seq', 'head'))
The draws below stay inside these ranges and needn't reach their ends.
Inputs may be any that keep to these rules, and one draw needn't show every extreme that they name: `window`: some head reaches 1 along both time and height, some head 0 along both.
All inputs are finite; a program needn't handle non-finite values.
Results may differ from the reference program's by a relative error of at most 0.0066.
Values may be sent and summed in bfloat16 or wider, within the bound.
No kernel may reach another device: no remote copies, remote signals or barrier semaphores. Data moves between devices by JAX's collectives and lax.ppermute only.
A program may use at most 128 MiB of HBM per device.

```python
import math
import jax
import jax.numpy as jnp
from jax import lax

H = 16
HD = 128
TILE = 384
GH = 4
TOKENS = 49152


def draw_queries(key, part):
    key = jax.random.fold_in(key, 1)
    noise = jnp.clip(jax.random.normal(key, (TOKENS, H * HD)), -6.0, 6.0)
    return noise.astype(jnp.bfloat16)


def draw_keys(key, part):
    key = jax.random.fold_in(key, 2)
    noise = jnp.clip(jax.random.normal(key, (TOKENS, H * HD)), -6.0, 6.0)
    return noise.astype(jnp.bfloat16)


def draw_window(key, part):
    key = jax.random.fold_in(key, 3)
    reaches = jax.random.randint(jax.random.fold_in(key, 1), (H, 2), 0, 2)
    head_order = jax.random.permutation(jax.random.fold_in(key, 2), H)
    reaches = reaches.at[head_order[0]].set(1)
    reaches = reaches.at[head_order[1]].set(0)
    return reaches.astype(jnp.int32)


def shard_levels(stream_key, extent, pieces, smallest, top_value):
    level, own = 1.0, jax.random.fold_in(stream_key, 6)
    for position, blocks in pieces:
        steps = jnp.exp(jax.random.uniform(jax.random.fold_in(own, position), (blocks,), jnp.float32, smallest / len(pieces), top_value / len(pieces)))
        level = level * jnp.repeat(steps, extent[position] // blocks).reshape([-1 if axis == position else 1 for axis in range(len(extent))])
    return level


def normal_values(key, extent, scale, limit, pieces=(), held_as=jnp.bfloat16):
    entries = jax.random.normal(key, extent, jnp.float32) * scale
    if len(pieces) > 0:
        entries = shard_levels(key, extent, pieces, -0.22, 0.18) * entries
    return jnp.clip(entries, min=-limit, max=limit).astype(held_as)


def setup_inputs(seed: int = 0) -> dict:
    arg_keys = jax.random.split(jax.random.key(seed), 6)
    return {
        "queries": draw_queries(jax.random.fold_in(arg_keys[5], 71), 0),
        "keys": draw_keys(jax.random.fold_in(arg_keys[5], 71), 0),
        "values": normal_values(arg_keys[2], (TOKENS, H * HD), 1.0, 6.0, ((0, 512),)),
        "out_grad": normal_values(arg_keys[3], (TOKENS, H * HD), 1.0, 6.0, ((0, 512),)),
        "window": draw_window(jax.random.fold_in(arg_keys[5], 71), 0),
    }


OFFSETS = tuple(((time_off, row_off) for time_off in (-1, 0, 1) for row_off in (-1, 0, 1)))

def reference(queries, keys, values, out_grad, window):
    tile_count = TOKENS // TILE
    slab_count = tile_count // 2
    grid_time = 2 * (slab_count // GH)
    score_scale = 1.0 / math.sqrt(HD)
    tile_ids = jnp.arange(tile_count, dtype=jnp.int32)
    slab_ids = tile_ids // 2
    tile_time = 2 * (slab_ids // GH) + tile_ids % 2
    tile_row = slab_ids % GH
    time_steps = jnp.array([pair[0] for pair in OFFSETS], dtype=jnp.int32)
    row_steps = jnp.array([pair[1] for pair in OFFSETS], dtype=jnp.int32)
    near_time = tile_time[:, None] + time_steps[None, :]
    near_row = tile_row[:, None] + row_steps[None, :]
    inside = (near_time >= 0) & (near_time < grid_time) & (near_row >= 0) & (near_row < GH)
    near_slab = near_time // 2 * GH + near_row
    neighbours = jnp.where(inside, 2 * near_slab + near_time % 2, 0).astype(jnp.int32)
    reach = (jnp.abs(time_steps)[None, :] <= window[:, 0:1]) & (jnp.abs(row_steps)[None, :] <= window[:, 1:2])
    tile_shape = (tile_count, TILE, H, HD)
    query_tiles = queries.reshape(tile_shape)
    key_tiles = keys.reshape(tile_shape)
    value_tiles = values.reshape(tile_shape)
    grad_tiles = out_grad.reshape(tile_shape)

    def one_tile(carry, tile_index):
        key_acc, value_acc = carry
        slots = neighbours[tile_index]
        visible = inside[tile_index][None, :] & reach
        query_here = query_tiles[tile_index].astype(jnp.float32)
        grad_here = grad_tiles[tile_index].astype(jnp.float32)
        key_near = key_tiles[slots].astype(jnp.float32)
        value_near = value_tiles[slots].astype(jnp.float32)
        scores = jnp.einsum('qnd,oknd->noqk', query_here, key_near) * score_scale
        scores = jnp.where(visible[:, :, None, None], scores, -jnp.inf)
        row_max = lax.optimization_barrier(jnp.max(scores, axis=(1, 3)))
        log_total = row_max + jnp.log(lax.optimization_barrier(jnp.sum(jnp.exp(scores - row_max[:, None, :, None]), axis=(1, 3))))
        weights = jnp.exp(scores - log_total[:, None, :, None])
        rounded = lax.optimization_barrier(weights.astype(jnp.bfloat16)).astype(jnp.float32)
        grad_scores = jnp.einsum('qnd,oknd->noqk', grad_here, value_near)
        row_delta = lax.optimization_barrier(jnp.sum(weights * grad_scores, axis=(1, 3)))
        dscore = (weights * (grad_scores - row_delta[:, None, :, None])).astype(jnp.bfloat16)
        dscore = lax.optimization_barrier(dscore).astype(jnp.float32)
        grad_query = jnp.einsum('noqk,oknd->qnd', dscore, key_near) * score_scale
        value_parts = jnp.einsum('noqk,qnd->oknd', rounded, grad_here)
        key_parts = jnp.einsum('noqk,qnd->oknd', dscore, query_here) * score_scale
        key_acc = key_acc.at[slots].add(key_parts)
        value_acc = value_acc.at[slots].add(value_parts)
        return ((key_acc, value_acc), grad_query.astype(jnp.bfloat16))
    zeros = jnp.zeros(tile_shape, jnp.float32)
    (key_acc, value_acc), grad_query = lax.scan(one_tile, (zeros, zeros), tile_ids)
    grad_queries = grad_query.reshape(TOKENS, H * HD)
    grad_keys = key_acc.astype(jnp.bfloat16).reshape(TOKENS, H * HD)
    grad_values = value_acc.astype(jnp.bfloat16).reshape(TOKENS, H * HD)
    return (grad_queries, grad_keys, grad_values)
```

```python
import functools

import jax
import jax.numpy as jnp
from jax import lax
from jax.experimental import pallas as pl
from jax.experimental.pallas import tpu as pltpu
from jax.sharding import Mesh, PartitionSpec as P

HD = 128
HEADS = 16
PIECE = 96
HALF = 192
TILE = 384
BF = jnp.bfloat16
F32 = jnp.float32
AXES = ("yl", "x", "zh", "zm", "zl", "yhh", "yhl", "c")
SIZES = (2, 4, 2, 2, 2, 2, 2, 2)
GROUP = ("zh", "yhh", "zl", "yhl")
Z = ("zh", "zm", "zl")
Z_PAIRS = [(1, 2), (2, 1), (5, 6), (6, 5), (0, 7), (7, 0), (4, 3), (3, 4)]
LINE = ("yl", "x")
FORTH = [(i, i + 1) for i in range(7)]
BACK = [(i + 1, i) for i in range(7)]
SWAP = [(0, 1), (1, 0)]
NEG = float("-inf")


def head_of(chip, zm):
    zh, yhh, zl, yhl = (chip // 8) % 2, (chip // 4) % 2, (chip // 2) % 2, chip % 2
    return ((zh * 2 + zl + zm) % 4) * 4 + yhh * 2 + yhl


def spread_kernel(zm_ref, a_ref, b_ref, out_ref):
    zm = zm_ref[0]
    for chip in range(HEADS):
        columns = pl.ds(pl.multiple_of(head_of(chip, zm) * HD, HD), HD)
        out_ref[chip, 0] = a_ref[:, columns]
        out_ref[chip, 1] = b_ref[:, columns]


def spread(zm, a, b):
    return pl.pallas_call(
        spread_kernel,
        out_shape=jax.ShapeDtypeStruct((HEADS, 2, PIECE, HD), BF),
        in_specs=[pl.BlockSpec(memory_space=pltpu.SMEM)] + [pl.BlockSpec(memory_space=pltpu.VMEM)] * 2,
        out_specs=pl.BlockSpec(memory_space=pltpu.VMEM),
        cost_estimate=pl.CostEstimate(flops=0, bytes_accessed=4 * 393216, transcendentals=0),
    )(zm, a, b)


def gather_kernel(count, zm_ref, in_ref, *out_refs):
    zm = zm_ref[0]
    for chip in range(HEADS):
        columns = pl.ds(pl.multiple_of(head_of(chip, zm) * HD, HD), HD)
        for n in range(count):
            out_refs[n][:, columns] = in_ref[chip, n]


def gather(zm, blocks):
    count = blocks.shape[1]
    return pl.pallas_call(
        functools.partial(gather_kernel, count),
        out_shape=[jax.ShapeDtypeStruct((PIECE, HEADS * HD), BF)] * count,
        in_specs=[pl.BlockSpec(memory_space=pltpu.SMEM), pl.BlockSpec(memory_space=pltpu.VMEM)],
        out_specs=[pl.BlockSpec(memory_space=pltpu.VMEM)] * count,
        cost_estimate=pl.CostEstimate(flops=0, bytes_accessed=2 * count * 393216, transcendentals=0),
    )(zm, blocks)


def dot(a, b, dims):
    return lax.dot_general(a, b, (dims, ((), ())), preferred_element_type=F32)


def attention_kernel(
    info, own, own_s, side, side_s, prev, prev_s, nxt, nxt_s, qg,
    dq_out, mine_out, sib_out,
    k_buf, v_buf, q_buf, g_buf, dk_acc, dv_acc, s_main, s_side, p_main, p_side, sems,
):
    zm, reach_t, reach_h = info[0], info[1], info[2]
    first_col, last_col = info[3], info[4]

    copies = []

    def copy(src, dst):
        c = pltpu.make_async_copy(src, dst, sems.at[len(copies)])
        c.start()
        copies.append(c)

    for zl in (0, 1):
        row = lax.rem(zm + zl, 2)
        copy(qg.at[:, zl, :, 0], q_buf.at[:, row])
        copy(qg.at[:, zl, :, 1], g_buf.at[:, row])
    for kv, buf in ((0, k_buf), (1, v_buf)):
        for core, (o, h, p, n) in enumerate(((own, side, prev, nxt), (own_s, side_s, prev_s, nxt_s))):
            for zl in (0, 1):
                row = lax.rem(zm + zl, 2)
                copy(o.at[:, zl, :, kv], buf.at[pl.ds(1, 4), row, core])
                copy(p.at[zl, :, kv], buf.at[0, row, core])
                copy(n.at[zl, :, kv], buf.at[5, row, core])
            copy(h.at[:, :, kv], buf.at[pl.ds(1, 4), 2, core])
            copy(p.at[2, :, kv], buf.at[0, 2, core])
            copy(n.at[2, :, kv], buf.at[5, 2, core])
    dk_acc[...] = jnp.zeros_like(dk_acc)
    dv_acc[...] = jnp.zeros_like(dv_acc)
    for c in copies:
        c.wait()

    scale2 = HD ** (-0.5) * 1.4426950408889634
    row_bias = jnp.where(reach_h >= 1, 0.0, NEG).astype(F32)
    block_row = lax.broadcasted_iota(jnp.int32, (TILE, 2 * TILE), 0) >= HALF
    block_col = lax.broadcasted_iota(jnp.int32, (TILE, 2 * TILE), 1) >= TILE
    main_bias = jnp.where(block_row == block_col, 0.0, row_bias)

    def keys(buf, col):
        return buf[col, 0:2].reshape(2 * TILE, HD), buf[col, 2].reshape(TILE, HD)

    def one_time(time, carry):
        q = q_buf[time].reshape(TILE, HD)
        g = g_buf[time].reshape(TILE, HD)
        q1, g1 = q[HALF:], g[HALF:]
        top_main, top_side = None, None
        for d in range(3):
            col = time + d
            allowed = (col >= first_col) & (col <= last_col) & ((reach_t >= 1) | (d == 1))
            time_bias = jnp.where(allowed, 0.0, NEG).astype(F32)
            k01, k2 = keys(k_buf, col)
            s = dot(q, k01, ((1,), (1,))) * scale2 + (main_bias + time_bias)
            s_main[d] = s
            t = jnp.max(s, axis=1, keepdims=True)
            top_main = t if top_main is None else jnp.maximum(top_main, t)
            s = dot(q1, k2, ((1,), (1,))) * scale2 + (row_bias + time_bias)
            s_side[d] = s
            t = jnp.max(s, axis=1, keepdims=True)
            top_side = t if top_side is None else jnp.maximum(top_side, t)
        top1 = jnp.maximum(top_main[HALF:], top_side)
        top = jnp.concatenate([top_main[:HALF], top1], axis=0)
        total = jnp.zeros((TILE, 1), F32)
        delta = jnp.zeros((TILE, 1), F32)
        total1 = jnp.zeros((HALF, 1), F32)
        delta1 = jnp.zeros((HALF, 1), F32)
        for d in range(3):
            v01, v2 = keys(v_buf, time + d)
            e = jnp.exp2(s_main[d] - top)
            p = dot(g, v01, ((1,), (1,)))
            s_main[d] = e
            p_main[d] = p
            total += jnp.sum(e, axis=1, keepdims=True)
            delta += jnp.sum(e * p, axis=1, keepdims=True)
            e = jnp.exp2(s_side[d] - top1)
            p = dot(g1, v2, ((1,), (1,)))
            s_side[d] = e
            p_side[d] = p
            total1 += jnp.sum(e, axis=1, keepdims=True)
            delta1 += jnp.sum(e * p, axis=1, keepdims=True)
        total = jnp.concatenate([total[:HALF], total[HALF:] + total1], axis=0)
        delta = jnp.concatenate([delta[:HALF], delta[HALF:] + delta1], axis=0)
        inverse = 1.0 / total
        delta = delta * inverse
        inverse1, delta1 = inverse[HALF:], delta[HALF:]
        qt, gt = q.T, g.T
        qt1, gt1 = q1.T, g1.T
        dq = jnp.zeros((TILE, HD), F32)
        dq1 = jnp.zeros((HALF, HD), F32)
        for d in range(3):
            col = time + d
            k01, k2 = keys(k_buf, col)
            w = s_main[d] * inverse
            ds = (w * (p_main[d] - delta)).astype(BF)
            w = w.astype(BF)
            dq += dot(ds, k01, ((1,), (0,)))
            dv_acc[col, :, 0 : 2 * TILE] += dot(gt, w, ((1,), (0,)))
            dk_acc[col, :, 0 : 2 * TILE] += dot(qt, ds, ((1,), (0,)))
            w = s_side[d] * inverse1
            ds = (w * (p_side[d] - delta1)).astype(BF)
            w = w.astype(BF)
            dq1 += dot(ds, k2, ((1,), (0,)))
            dv_acc[col, :, 2 * TILE : 3 * TILE] += dot(gt1, w, ((1,), (0,)))
            dk_acc[col, :, 2 * TILE : 3 * TILE] += dot(qt1, ds, ((1,), (0,)))
        dq = jnp.concatenate([dq[:HALF], dq[HALF:] + dq1], axis=0) * HD ** (-0.5)
        for row in (0, 1):
            zl = lax.rem(zm + row, 2)
            dq_out[time, zl] = dq[row * HALF : (row + 1) * HALF].astype(BF).reshape(2, PIECE, HD)
        return carry

    lax.fori_loop(0, 4, one_time, 0)

    def place(base, kv, block):
        for core, out in ((0, mine_out), (1, sib_out)):
            for yhl in (0, 1):
                start = core * HALF + yhl * PIECE
                out[base + yhl * 2 + kv] = block[start : start + PIECE]

    def finish(col, base0, base1, base2):
        for kv, acc, factor in ((0, dk_acc, HD ** (-0.5)), (1, dv_acc, 1.0)):
            whole = (acc[col] * factor).astype(BF).T
            place(base0, kv, whole[:TILE])
            place(base1, kv, whole[TILE : 2 * TILE])
            place(base2, kv, whole[2 * TILE :])

    zl0, zl1 = zm, 1 - zm

    def finish_own(time, carry):
        finish(time + 1, time * 8 + zl0 * 4, time * 8 + zl1 * 4, 32 + time * 4)
        return carry

    lax.fori_loop(0, 4, finish_own, 0)
    finish(0, 48 + zl0 * 4, 48 + zl1 * 4, 48 + 8)
    finish(5, 60 + zl0 * 4, 60 + zl1 * 4, 60 + 8)


def attention(info, *arrays):
    return pl.pallas_call(
        attention_kernel,
        out_shape=[
            jax.ShapeDtypeStruct((4, 2, 2, PIECE, HD), BF),
            jax.ShapeDtypeStruct((72, PIECE, HD), BF),
            jax.ShapeDtypeStruct((72, PIECE, HD), BF),
        ],
        in_specs=[pl.BlockSpec(memory_space=pltpu.SMEM)] + [pl.BlockSpec(memory_space=pl.ANY)] * 9,
        out_specs=[pl.BlockSpec(memory_space=pltpu.VMEM)] * 3,
        scratch_shapes=[
            pltpu.VMEM((6, 3, 2, 2, PIECE, HD), BF),
            pltpu.VMEM((6, 3, 2, 2, PIECE, HD), BF),
            pltpu.VMEM((4, 2, 2, PIECE, HD), BF),
            pltpu.VMEM((4, 2, 2, PIECE, HD), BF),
            pltpu.VMEM((6, HD, 3 * TILE), F32),
            pltpu.VMEM((6, HD, 3 * TILE), F32),
            pltpu.VMEM((3, TILE, 2 * TILE), F32),
            pltpu.VMEM((3, HALF, TILE), F32),
            pltpu.VMEM((3, TILE, 2 * TILE), F32),
            pltpu.VMEM((3, HALF, TILE), F32),
            pltpu.SemaphoreType.DMA((40,)),
        ],
        compiler_params=pltpu.CompilerParams(vmem_limit_bytes=48 * 1024 * 1024),
        cost_estimate=pl.CostEstimate(flops=6 * 10**9, bytes_accessed=9 * 10**6, transcendentals=5 * 10**6),
    )(info, *arrays)


def to_heads(blocks):
    return lax.all_to_all(blocks, GROUP, split_axis=0, concat_axis=0, tiled=True)


def swapped(block):
    return lax.ppermute(block, "c", SWAP)


def per_device(queries, keys, values, out_grad, window):
    at = {name: lax.axis_index(name) for name in AXES}
    zm = at["zm"]
    zm_arg = jnp.full((1,), zm, jnp.int32)
    place = at["yl"] * 4 + at["x"]
    chip = ((at["zh"] * 2 + at["yhh"]) * 2 + at["zl"]) * 2 + at["yhl"]
    reach = lax.dynamic_slice_in_dim(window, head_of(chip, zm), 1, 0)[0]
    info = jnp.stack(
        [zm, reach[0], reach[1], jnp.where(place == 0, 1, 0), jnp.where(place == 7, 4, 5)]
    ).astype(jnp.int32)

    own = to_heads(spread(zm_arg, keys, values)).reshape(4, 2, 2, 2, PIECE, HD)
    qg = to_heads(spread(zm_arg, queries, out_grad)).reshape(4, 2, 2, 2, PIECE, HD)
    own_s = swapped(own)
    inner = lax.dynamic_slice_in_dim(own, 1 - zm, 1, 1)[:, 0]
    side = lax.ppermute(inner, Z, Z_PAIRS)
    nxt = lax.ppermute(jnp.concatenate([own[0], side[:1]], axis=0), LINE, BACK)
    prev = lax.ppermute(jnp.concatenate([own[3], side[3:]], axis=0), LINE, FORTH)
    dq, mine, sib = attention(
        info, own, own_s, side, swapped(side), prev, swapped(prev), nxt, swapped(nxt), qg
    )
    grad_queries = gather(zm_arg, to_heads(dq.reshape(HEADS, 1, PIECE, HD)))[0]
    terms = mine.astype(F32) + swapped(sib).astype(F32)
    d_own = terms[:32].reshape(4, 2, 2, 2, PIECE, HD)
    d_side = terms[32:48].reshape(4, 2, 2, PIECE, HD)
    d_prev = terms[48:60].reshape(3, 2, 2, PIECE, HD).astype(BF)
    d_nxt = terms[60:72].reshape(3, 2, 2, PIECE, HD).astype(BF)
    to_last = lax.ppermute(d_prev, LINE, BACK).astype(F32)
    to_first = lax.ppermute(d_nxt, LINE, FORTH).astype(F32)
    d_side = d_side.at[0].add(to_first[2]).at[3].add(to_last[2])
    to_inner = lax.ppermute(d_side.astype(BF), Z, Z_PAIRS).astype(F32)
    d_own = d_own.at[0].add(to_first[:2]).at[3].add(to_last[:2])
    is_inner = (jnp.arange(2) == 1 - zm)[None, :, None, None, None, None]
    d_own = d_own + jnp.where(is_inner, to_inner[:, None], 0.0)
    d_own = d_own.astype(BF).reshape(HEADS, 2, PIECE, HD)
    grad_keys, grad_values = gather(zm_arg, to_heads(d_own))
    return grad_queries, grad_keys, grad_values


def solution(mesh):
    fine = Mesh(mesh.devices.reshape(SIZES), AXES)
    rows = P(AXES, None)
    return jax.shard_map(
        per_device,
        mesh=fine,
        in_specs=(rows, rows, rows, rows, P()),
        out_specs=(rows, rows, rows),
        check_vma=False,
    )
```

```python
import functools

import jax
import jax.numpy as jnp
from jax import lax
from jax.experimental import pallas as pl
from jax.experimental.pallas import tpu as pltpu
from jax.sharding import Mesh, PartitionSpec as P

HD = 128
HEADS = 16
PIECE = 96
HALF = 192
TILE = 384
BF = jnp.bfloat16
F32 = jnp.float32
AXES = ("yl", "x", "zh", "zm", "zl", "yhh", "yhl", "c")
SIZES = (2, 4, 2, 2, 2, 2, 2, 2)
GROUP = ("zh", "yhh", "zl", "yhl")
Z = ("zh", "zm", "zl")
Z_PAIRS = [(1, 2), (2, 1), (5, 6), (6, 5), (0, 7), (7, 0), (4, 3), (3, 4)]
LINE = ("yl", "x")
FORTH = [(i, i + 1) for i in range(7)]
BACK = [(i + 1, i) for i in range(7)]
SWAP = [(0, 1), (1, 0)]
NEG = float("-inf")


def head_of(chip, zm):
    zh, yhh, zl, yhl = (chip // 8) % 2, (chip // 4) % 2, (chip // 2) % 2, chip % 2
    return ((zh * 2 + zl + zm) % 4) * 4 + yhh * 2 + yhl


def spread_kernel(zm_ref, a_ref, b_ref, out_ref):
    zm = zm_ref[0]
    for chip in range(HEADS):
        columns = pl.ds(pl.multiple_of(head_of(chip, zm) * HD, HD), HD)
        out_ref[chip, 0] = a_ref[:, columns]
        out_ref[chip, 1] = b_ref[:, columns]


def spread(zm, a, b):
    return pl.pallas_call(
        spread_kernel,
        out_shape=jax.ShapeDtypeStruct((HEADS, 2, PIECE, HD), BF),
        in_specs=[pl.BlockSpec(memory_space=pltpu.SMEM)] + [pl.BlockSpec(memory_space=pltpu.VMEM)] * 2,
        out_specs=pl.BlockSpec(memory_space=pltpu.VMEM),
        cost_estimate=pl.CostEstimate(flops=0, bytes_accessed=4 * 393216, transcendentals=0),
    )(zm, a, b)


def gather_kernel(count, zm_ref, in_ref, *out_refs):
    zm = zm_ref[0]
    for chip in range(HEADS):
        columns = pl.ds(pl.multiple_of(head_of(chip, zm) * HD, HD), HD)
        for n in range(count):
            out_refs[n][:, columns] = in_ref[chip, n]


def gather(zm, blocks):
    count = blocks.shape[1]
    return pl.pallas_call(
        functools.partial(gather_kernel, count),
        out_shape=[jax.ShapeDtypeStruct((PIECE, HEADS * HD), BF)] * count,
        in_specs=[pl.BlockSpec(memory_space=pltpu.SMEM), pl.BlockSpec(memory_space=pltpu.VMEM)],
        out_specs=[pl.BlockSpec(memory_space=pltpu.VMEM)] * count,
        cost_estimate=pl.CostEstimate(flops=0, bytes_accessed=2 * count * 393216, transcendentals=0),
    )(zm, blocks)


def dot(a, b, dims):
    return lax.dot_general(a, b, (dims, ((), ())), preferred_element_type=F32)


def attention_kernel(
    zm_ref, chip_ref, line_ref, window_ref, own, own_s, side, side_s, prev, prev_s, nxt, nxt_s, qg,
    dq_out, mine_out, sib_out,
    k_buf, v_buf, q_buf, g_buf, dk_acc, dv_acc, s_main, s_side, p_main, p_side, sems,
):
    zm, line = zm_ref[0], line_ref[0]
    head = head_of(chip_ref[0], zm)
    reach_t, reach_h = window_ref[head, 0], window_ref[head, 1]
    first_col = jnp.where(line == 0, 1, 0)
    last_col = jnp.where(line == 7, 4, 5)
    zls = (zm, 1 - zm)
    copies = []

    def copy(src, dst):
        c = pltpu.make_async_copy(src, dst, sems.at[len(copies)])
        c.start()
        copies.append(c)

    for kv, buf, part in ((0, k_buf, q_buf), (1, v_buf, g_buf)):
        for row in (0, 1):
            copy(qg.at[:, zls[row], :, kv], part.at[:, row])
        for core, (o, h, p, n) in enumerate(((own, side, prev, nxt), (own_s, side_s, prev_s, nxt_s))):
            for row in (0, 1):
                copy(o.at[:, zls[row], :, kv], buf.at[pl.ds(1, 4), row, core])
                copy(p.at[zls[row], :, kv], buf.at[0, row, core])
                copy(n.at[zls[row], :, kv], buf.at[5, row, core])
            copy(h.at[:, :, kv], buf.at[pl.ds(1, 4), 2, core])
            copy(p.at[2, :, kv], buf.at[0, 2, core])
            copy(n.at[2, :, kv], buf.at[5, 2, core])
    dk_acc[0:2] = jnp.zeros((2,) + dk_acc.shape[1:], F32)
    dv_acc[0:2] = jnp.zeros((2,) + dv_acc.shape[1:], F32)
    for c in copies:
        c.wait()

    scale2 = HD ** (-0.5) * 1.4426950408889634
    row_bias = jnp.where(reach_h >= 1, 0.0, NEG).astype(F32)

    def keys(buf, col):
        return buf[col, 0:2].reshape(2 * TILE, HD), buf[col, 2].reshape(TILE, HD)

    def lanes(j):
        return slice(j * 128, (j + 1) * 128)

    def finish(col, kv, block):
        block = (block * (1.0 if kv else HD ** (-0.5))).astype(BF).T
        for row in range(3):
            place = 2 if row == 2 else zls[row]
            for core, out in ((0, mine_out), (1, sib_out)):
                for yhl in (0, 1):
                    start = row * TILE + core * HALF + yhl * PIECE
                    out[col, place, yhl, kv] = block[start : start + PIECE]

    def one_time(time, carry):
        q = q_buf[time].reshape(TILE, HD)
        g = g_buf[time].reshape(TILE, HD)
        q1, g1 = q[HALF:], g[HALF:]
        tops = [jnp.full((HALF, 128), NEG, F32)] * 2
        for d in range(3):
            col = time + d
            allowed = (col >= first_col) & (col <= last_col) & ((reach_t >= 1) | (d == 1))
            time_bias = jnp.where(allowed, 0.0, NEG).astype(F32)
            far_bias = time_bias + row_bias
            k01, k2 = keys(k_buf, col)
            s = dot(q, k01, ((1,), (1,))) * scale2
            for half in (0, 1):
                for j in range(6):
                    part = s[half * HALF : (half + 1) * HALF, lanes(j)]
                    if j // 3 != half:
                        part = part + far_bias
                    elif d != 1:
                        part = part + time_bias
                    s_main[d, half * HALF : (half + 1) * HALF, lanes(j)] = part
                    tops[half] = jnp.maximum(tops[half], part)
            s = dot(q1, k2, ((1,), (1,))) * scale2 + far_bias
            s_side[d] = s
            for j in range(3):
                tops[1] = jnp.maximum(tops[1], s[:, lanes(j)])
        tops = [jnp.max(t, axis=1, keepdims=True) for t in tops]
        top = jnp.concatenate(tops, axis=0)
        total = jnp.zeros((TILE, 128), F32)
        delta = jnp.zeros((TILE, 128), F32)
        total1 = jnp.zeros((HALF, 128), F32)
        delta1 = jnp.zeros((HALF, 128), F32)
        for d in range(3):
            v01, v2 = keys(v_buf, time + d)
            p = dot(g, v01, ((1,), (1,)))
            p_main[d] = p
            for j in range(6):
                e = jnp.exp2(s_main[d, :, lanes(j)] - top)
                s_main[d, :, lanes(j)] = e
                total += e
                delta += e * p[:, lanes(j)]
            p = dot(g1, v2, ((1,), (1,)))
            p_side[d] = p
            for j in range(3):
                e = jnp.exp2(s_side[d, :, lanes(j)] - tops[1])
                s_side[d, :, lanes(j)] = e
                total1 += e
                delta1 += e * p[:, lanes(j)]
        total = jnp.concatenate([total[:HALF], total[HALF:] + total1], axis=0)
        delta = jnp.concatenate([delta[:HALF], delta[HALF:] + delta1], axis=0)
        inverse = 1.0 / jnp.sum(total, axis=1, keepdims=True)
        delta = jnp.sum(delta, axis=1, keepdims=True) * inverse
        qt, gt = q.T, g.T
        qt1, gt1 = qt[:, HALF:], gt[:, HALF:]
        dq = jnp.zeros((TILE, HD), F32)
        dq1 = jnp.zeros((HALF, HD), F32)
        for d in range(3):
            col = time + d
            k01, k2 = keys(k_buf, col)
            w = s_main[d] * inverse
            ds = (w * (p_main[d] - delta)).astype(BF)
            w1 = s_side[d] * inverse[HALF:]
            ds1 = (w1 * (p_side[d] - delta[HALF:])).astype(BF)
            dq += dot(ds, k01, ((1,), (0,)))
            dq1 += dot(ds1, k2, ((1,), (0,)))
            for kv, acc, main, last in ((0, dk_acc, dot(qt, ds, ((1,), (0,))), dot(qt1, ds1, ((1,), (0,)))),
                                  (1, dv_acc, dot(gt, w.astype(BF), ((1,), (0,))), dot(gt1, w1.astype(BF), ((1,), (0,))))):
                if d == 2:
                    acc[col, :, 0 : 2 * TILE] = main
                    acc[col, :, 2 * TILE :] = last
                elif d == 1:
                    acc[col, :, 0 : 2 * TILE] += main
                    acc[col, :, 2 * TILE :] += last
                else:
                    finish(col, kv, acc[col] + jnp.concatenate([main, last], axis=1))
        dq = jnp.concatenate([dq[:HALF], dq[HALF:] + dq1], axis=0) * (HD ** (-0.5))
        for row in (0, 1):
            dq_out[time, zls[row]] = dq[row * HALF : (row + 1) * HALF].astype(BF).reshape(2, PIECE, HD)
        return carry

    lax.fori_loop(0, 4, one_time, 0, unroll=1)
    for col in (4, 5):
        finish(col, 0, dk_acc[col])
        finish(col, 1, dv_acc[col])


def attention(*arrays):
    return pl.pallas_call(
        attention_kernel,
        out_shape=[
            jax.ShapeDtypeStruct((4, 2, 2, PIECE, HD), BF),
            jax.ShapeDtypeStruct((6, 3, 2, 2, PIECE, HD), BF),
            jax.ShapeDtypeStruct((6, 3, 2, 2, PIECE, HD), BF),
        ],
        in_specs=[pl.BlockSpec(memory_space=pltpu.SMEM)] * 4 + [pl.BlockSpec(memory_space=pl.ANY)] * 9,
        out_specs=[pl.BlockSpec(memory_space=pltpu.VMEM)] * 3,
        scratch_shapes=[
            pltpu.VMEM((6, 3, 2, 2, PIECE, HD), BF),
            pltpu.VMEM((6, 3, 2, 2, PIECE, HD), BF),
            pltpu.VMEM((4, 2, 2, PIECE, HD), BF),
            pltpu.VMEM((4, 2, 2, PIECE, HD), BF),
            pltpu.VMEM((6, HD, 3 * TILE), F32),
            pltpu.VMEM((6, HD, 3 * TILE), F32),
            pltpu.VMEM((3, TILE, 2 * TILE), F32),
            pltpu.VMEM((3, HALF, TILE), F32),
            pltpu.VMEM((3, TILE, 2 * TILE), F32),
            pltpu.VMEM((3, HALF, TILE), F32),
            pltpu.SemaphoreType.DMA((40,)),
        ],
        compiler_params=pltpu.CompilerParams(vmem_limit_bytes=48 * 1024 * 1024),
        cost_estimate=pl.CostEstimate(flops=6 * 10**9, bytes_accessed=9 * 10**6, transcendentals=5 * 10**6),
    )(*arrays)


def to_heads(blocks):
    return lax.all_to_all(blocks, GROUP, split_axis=0, concat_axis=0, tiled=True)


def swapped(block):
    return lax.ppermute(block, "c", SWAP)


def scalar(value):
    return jnp.full((1,), value, jnp.int32)


def per_device(queries, keys, values, out_grad, window):
    at = {name: lax.axis_index(name) for name in AXES}
    zm = at["zm"]
    zm_arg = scalar(zm)
    line = scalar(at["yl"] * 4 + at["x"])
    chip = scalar(((at["zh"] * 2 + at["yhh"]) * 2 + at["zl"]) * 2 + at["yhl"])

    own = to_heads(spread(zm_arg, keys, values)).reshape(4, 2, 2, 2, PIECE, HD)
    inner = lax.dynamic_slice_in_dim(own, 1 - zm, 1, 1)[:, 0]
    qg = spread(zm_arg, queries, out_grad)
    side = lax.ppermute(inner, Z, Z_PAIRS)
    qg, side = lax.optimization_barrier((qg, side))
    qg = to_heads(qg).reshape(4, 2, 2, 2, PIECE, HD)
    own_s = swapped(own)
    nxt = lax.ppermute(jnp.concatenate([own[0], side[:1]], axis=0), LINE, BACK)
    prev = lax.ppermute(jnp.concatenate([own[3], side[3:]], axis=0), LINE, FORTH)
    dq, mine, sib = attention(
        zm_arg, chip, line, window, own, own_s, side, swapped(side), prev, swapped(prev), nxt, swapped(nxt), qg
    )
    sib = swapped(sib)

    def terms(*at):
        return mine[at].astype(F32) + sib[at].astype(F32)

    to_last = lax.ppermute(terms(0).astype(BF), LINE, BACK)
    to_first = lax.ppermute(terms(5).astype(BF), LINE, FORTH)
    d_side = [terms(time + 1, 2) for time in range(4)]
    d_side[0] += to_first[2].astype(F32)
    d_side[3] += to_last[2].astype(F32)
    to_inner = lax.ppermute(jnp.stack(d_side).astype(BF), Z, Z_PAIRS)
    is_inner = (jnp.arange(2) == 1 - zm)[:, None, None, None, None]
    d_own = []
    for time in range(4):
        total = terms(time + 1, slice(0, 2)) + jnp.where(is_inner, to_inner[time][None].astype(F32), 0.0)
        if time == 0:
            total = total + to_first[:2].astype(F32)
        if time == 3:
            total = total + to_last[:2].astype(F32)
        d_own.append(total.astype(BF))
    grads = jnp.concatenate([jnp.stack(d_own), dq[:, :, :, None]], axis=3).reshape(HEADS, 3, PIECE, HD)
    grad_keys, grad_values, grad_queries = gather(zm_arg, to_heads(grads))
    return grad_queries, grad_keys, grad_values


def solution(mesh):
    fine = Mesh(mesh.devices.reshape(SIZES), AXES)
    rows = P(AXES, None)
    return jax.shard_map(
        per_device,
        mesh=fine,
        in_specs=(rows, rows, rows, rows, P()),
        out_specs=(rows, rows, rows),
        check_vma=False,
    )
```

```python
import functools

import jax
import jax.numpy as jnp
from jax import lax
from jax.experimental import pallas as pl
from jax.experimental.pallas import tpu as pltpu
from jax.sharding import Mesh, PartitionSpec as P

HD = 128
HEADS = 16
PIECE = 96
HALF = 192
TILE = 384
BF = jnp.bfloat16
F32 = jnp.float32
AXES = ("yl", "x", "zh", "zm", "zl", "yhh", "yhl", "c")
SIZES = (2, 4, 2, 2, 2, 2, 2, 2)
GROUP = ("zh", "yhh", "zl", "yhl")
Z = ("zh", "zm", "zl")
Z_PAIRS = [(1, 2), (2, 1), (5, 6), (6, 5), (0, 7), (7, 0), (4, 3), (3, 4)]
LINE = ("yl", "x")
FORTH = [(i, i + 1) for i in range(7)]
BACK = [(i + 1, i) for i in range(7)]
SWAP = [(0, 1), (1, 0)]
NEG = float("-inf")


def head_of(chip, zm):
    zh, yhh, zl, yhl = (chip // 8) % 2, (chip // 4) % 2, (chip // 2) % 2, chip % 2
    return ((zh * 2 + zl + zm) % 4) * 4 + yhh * 2 + yhl


def spread_kernel(zm_ref, a_ref, b_ref, out_ref):
    zm = zm_ref[0]
    for chip in range(HEADS):
        columns = pl.ds(pl.multiple_of(head_of(chip, zm) * HD, HD), HD)
        out_ref[chip, 0] = a_ref[:, columns]
        out_ref[chip, 1] = b_ref[:, columns]


def spread(zm, a, b):
    return pl.pallas_call(
        spread_kernel,
        out_shape=jax.ShapeDtypeStruct((HEADS, 2, PIECE, HD), BF),
        in_specs=[pl.BlockSpec(memory_space=pltpu.SMEM)] + [pl.BlockSpec(memory_space=pltpu.VMEM)] * 2,
        out_specs=pl.BlockSpec(memory_space=pltpu.VMEM),
        cost_estimate=pl.CostEstimate(flops=0, bytes_accessed=4 * 393216, transcendentals=0),
    )(zm, a, b)


def gather_kernel(count, zm_ref, in_ref, *out_refs):
    zm = zm_ref[0]
    for chip in range(HEADS):
        columns = pl.ds(pl.multiple_of(head_of(chip, zm) * HD, HD), HD)
        for n in range(count):
            out_refs[n][:, columns] = in_ref[chip, n]


def gather(zm, blocks):
    count = blocks.shape[1]
    return pl.pallas_call(
        functools.partial(gather_kernel, count),
        out_shape=[jax.ShapeDtypeStruct((PIECE, HEADS * HD), BF)] * count,
        in_specs=[pl.BlockSpec(memory_space=pltpu.SMEM), pl.BlockSpec(memory_space=pltpu.VMEM)],
        out_specs=[pl.BlockSpec(memory_space=pltpu.VMEM)] * count,
        cost_estimate=pl.CostEstimate(flops=0, bytes_accessed=2 * count * 393216, transcendentals=0),
    )(zm, blocks)


def dot(a, b, dims):
    return lax.dot_general(a, b, (dims, ((), ())), preferred_element_type=F32)


def attention_kernel(
    zm_ref, chip_ref, line_ref, window_ref, own, own_s, side, side_s, prev, prev_s, nxt, nxt_s, qg,
    dq_out, mine_out, sib_edge, sib_mid,
    k_buf, v_buf, q_buf, g_buf, dk_acc, dv_acc, s_main, s_side, p_main, p_side, sems,
):
    zm, line = zm_ref[0], line_ref[0]
    head = head_of(chip_ref[0], zm)
    reach_t, reach_h = window_ref[head, 0], window_ref[head, 1]
    first_col = jnp.where(line == 0, 1, 0)
    last_col = jnp.where(line == 7, 4, 5)
    zls = (zm, 1 - zm)
    copies = []

    def copy(src, dst):
        c = pltpu.make_async_copy(src, dst, sems.at[len(copies)])
        c.start()
        copies.append(c)

    for kv, buf, part in ((0, k_buf, q_buf), (1, v_buf, g_buf)):
        copy(qg.at[:, :, :, kv], part)
        for core, (o, h, p, n) in enumerate(((own, side, prev, nxt), (own_s, side_s, prev_s, nxt_s))):
            copy(o.at[:, :, :, kv], buf.at[pl.ds(1, 4), pl.ds(0, 2), core])
            copy(h.at[:, :, kv], buf.at[pl.ds(1, 4), 2, core])
            copy(p.at[:, :, kv], buf.at[0, :, core])
            copy(n.at[:, :, kv], buf.at[5, :, core])
    for c in copies[: len(copies) // 2]:
        c.wait()

    scale2 = HD ** (-0.5) * 1.4426950408889634
    row_bias = jnp.where(reach_h >= 1, 0.0, NEG).astype(F32)

    def keys(buf, col):
        edge, inner, side = (buf[col, row].reshape(TILE, HD) for row in (*zls, 2))
        return jnp.concatenate([edge, inner], axis=0), side

    def queries(buf, time):
        return jnp.concatenate([buf[time, zl].reshape(HALF, HD) for zl in zls], axis=0)

    def lanes(j):
        return slice(j * 128, (j + 1) * 128)

    def finish(col, kv, block):
        block = (block * (1.0 if kv else HD ** (-0.5))).astype(BF).T
        for row in range(3):
            place = 2 if row == 2 else zls[row]
            sib, at = (sib_edge, col // 5) if col in (0, 5) else (sib_mid, col - 1)
            for core, out, at in ((0, mine_out, col), (1, sib, at)):
                for yhl in (0, 1):
                    start = row * TILE + core * HALF + yhl * PIECE
                    out[at, place, yhl, kv] = block[start : start + PIECE]

    def scores(time, d, slot, tops):
        col = time + d
        allowed = (col >= first_col) & (col <= last_col) & ((reach_t >= 1) | (d == 1))
        time_bias = jnp.where(allowed, 0.0, NEG).astype(F32)
        far_bias = time_bias + row_bias
        tops = list(tops)
        q = queries(q_buf, time)
        k01, k2 = keys(k_buf, col)
        s = dot(q, k01, ((1,), (1,))) * scale2
        for half in (0, 1):
            for j in range(6):
                part = s[half * HALF : (half + 1) * HALF, lanes(j)]
                if j // 3 != half:
                    part = part + far_bias
                elif d != 1:
                    part = part + time_bias
                s_main[slot, d, half * HALF : (half + 1) * HALF, lanes(j)] = part
                tops[half] = jnp.maximum(tops[half], part)
        s = dot(q[HALF:], k2, ((1,), (1,))) * scale2 + far_bias
        s_side[slot, d] = s
        for j in range(3):
            tops[1] = jnp.maximum(tops[1], s[:, lanes(j)])
        return tuple(tops)

    no_tops = (jnp.full((HALF, 128), NEG, F32),) * 2

    def one_time(time, slot, tops, after):
        q = queries(q_buf, time)
        g = queries(g_buf, time)
        g1 = g[HALF:]
        tops = [jnp.max(t, axis=1, keepdims=True) for t in tops]
        top = jnp.concatenate(tops, axis=0)
        total = jnp.zeros((TILE, 128), F32)
        delta = jnp.zeros((TILE, 128), F32)
        total1 = jnp.zeros((HALF, 128), F32)
        delta1 = jnp.zeros((HALF, 128), F32)
        for d in range(3):
            v01, v2 = keys(v_buf, time + d)
            p = dot(g, v01, ((1,), (1,)))
            p_main[d] = p
            for j in range(6):
                e = jnp.exp2(s_main[slot, d, :, lanes(j)] - top)
                s_main[slot, d, :, lanes(j)] = e
                total += e
                delta += e * p[:, lanes(j)]
            p = dot(g1, v2, ((1,), (1,)))
            p_side[d] = p
            for j in range(3):
                e = jnp.exp2(s_side[slot, d, :, lanes(j)] - tops[1])
                s_side[slot, d, :, lanes(j)] = e
                total1 += e
                delta1 += e * p[:, lanes(j)]
        total = jnp.concatenate([total[:HALF], total[HALF:] + total1], axis=0)
        delta = jnp.concatenate([delta[:HALF], delta[HALF:] + delta1], axis=0)
        inverse = 1.0 / jnp.sum(total, axis=1, keepdims=True)
        delta = jnp.sum(delta, axis=1, keepdims=True) * inverse
        qt, gt = q.T, g.T
        qt1, gt1 = qt[:, HALF:], gt[:, HALF:]
        dq = jnp.zeros((TILE, HD), F32)
        dq1 = jnp.zeros((HALF, HD), F32)
        next_tops = no_tops
        for d in range(3):
            col = time + d
            if after is not None:
                next_tops = scores(after, d, 1 - slot, next_tops)
            k01, k2 = keys(k_buf, col)
            w = s_main[slot, d] * inverse
            ds = (w * (p_main[d] - delta)).astype(BF)
            w1 = s_side[slot, d] * inverse[HALF:]
            ds1 = (w1 * (p_side[d] - delta[HALF:])).astype(BF)
            dq += dot(ds, k01, ((1,), (0,)))
            dq1 += dot(ds1, k2, ((1,), (0,)))
            main_k, last_k = dot(qt, ds, ((1,), (0,))), dot(qt1, ds1, ((1,), (0,)))
            main_v, last_v = dot(gt, w.astype(BF), ((1,), (0,))), dot(gt1, w1.astype(BF), ((1,), (0,)))
            for kv, acc, main, last in ((0, dk_acc, main_k, last_k), (1, dv_acc, main_v, last_v)):
                if d == 2 or (time == 0 and d == 1):
                    acc[col, :, 0 : 2 * TILE] = main
                    acc[col, :, 2 * TILE :] = last
                elif d == 1:
                    acc[col, :, 0 : 2 * TILE] += main
                    acc[col, :, 2 * TILE :] += last
                else:
                    block = jnp.concatenate([main, last], axis=1)
                    finish(col, kv, block if time == 0 else block + acc[col])
        dq = jnp.concatenate([dq[:HALF], dq[HALF:] + dq1], axis=0) * HD ** (-0.5)
        for row in (0, 1):
            dq_out[time, zls[row]] = dq[row * HALF : (row + 1) * HALF].astype(BF).reshape(2, PIECE, HD)
        return next_tops

    tops = no_tops
    for d in range(3):
        tops = scores(0, d, 0, tops)
    for c in copies[len(copies) // 2 :]:
        c.wait()

    for time in range(4):
        tops = one_time(time, time % 2, tops, time + 1 if time < 3 else None)
    for col in (4, 5):
        finish(col, 0, dk_acc[col])
        finish(col, 1, dv_acc[col])


def attention(*arrays):
    return pl.pallas_call(
        attention_kernel,
        out_shape=[
            jax.ShapeDtypeStruct((4, 2, 2, PIECE, HD), BF),
            jax.ShapeDtypeStruct((6, 3, 2, 2, PIECE, HD), BF),
            jax.ShapeDtypeStruct((2, 3, 2, 2, PIECE, HD), BF),
            jax.ShapeDtypeStruct((4, 3, 2, 2, PIECE, HD), BF),
        ],
        in_specs=[pl.BlockSpec(memory_space=pltpu.SMEM)] * 4 + [pl.BlockSpec(memory_space=pl.ANY)] * 9,
        out_specs=[pl.BlockSpec(memory_space=pltpu.VMEM)] * 4,
        scratch_shapes=[
            pltpu.VMEM((6, 3, 2, 2, PIECE, HD), BF),
            pltpu.VMEM((6, 3, 2, 2, PIECE, HD), BF),
            pltpu.VMEM((4, 2, 2, PIECE, HD), BF),
            pltpu.VMEM((4, 2, 2, PIECE, HD), BF),
            pltpu.VMEM((6, HD, 3 * TILE), F32),
            pltpu.VMEM((6, HD, 3 * TILE), F32),
            pltpu.VMEM((2, 3, TILE, 2 * TILE), F32),
            pltpu.VMEM((2, 3, HALF, TILE), F32),
            pltpu.VMEM((3, TILE, 2 * TILE), F32),
            pltpu.VMEM((3, HALF, TILE), F32),
            pltpu.SemaphoreType.DMA((18,)),
        ],
        compiler_params=pltpu.CompilerParams(vmem_limit_bytes=48 * 1024 * 1024),
        cost_estimate=pl.CostEstimate(flops=6 * 10**9, bytes_accessed=9 * 10**6, transcendentals=5 * 10**6),
    )(*arrays)


def to_heads(blocks):
    return lax.all_to_all(blocks, GROUP, split_axis=0, concat_axis=0, tiled=True)


def swapped(block):
    return lax.ppermute(block, "c", SWAP)


def scalar(value):
    return jnp.full((1,), value, jnp.int32)


def per_device(queries, keys, values, out_grad, window):
    at = {name: lax.axis_index(name) for name in AXES}
    zm = at["zm"]
    zm_arg = scalar(zm)
    line = scalar(at["yl"] * 4 + at["x"])
    chip = scalar(((at["zh"] * 2 + at["yhh"]) * 2 + at["zl"]) * 2 + at["yhl"])

    own = to_heads(spread(zm_arg, keys, values)).reshape(4, 2, 2, 2, PIECE, HD)
    inner = lax.dynamic_slice_in_dim(own, 1 - zm, 1, 1)[:, 0]
    qg = spread(zm_arg, queries, out_grad)
    side = lax.ppermute(inner, Z, Z_PAIRS)
    qg, side = lax.optimization_barrier((qg, side))
    qg = to_heads(qg).reshape(4, 2, 2, 2, PIECE, HD)
    own_s = swapped(own)
    nxt = lax.ppermute(jnp.concatenate([own[0], side[:1]], axis=0), LINE, BACK)
    prev = lax.ppermute(jnp.concatenate([own[3], side[3:]], axis=0), LINE, FORTH)
    dq, mine, sib_edge, sib_mid = attention(
        zm_arg, chip, line, window, own, own_s, side, swapped(side), prev, swapped(prev), nxt, swapped(nxt), qg
    )
    sib_edge = swapped(sib_edge)
    d_prev = (mine[0].astype(F32) + sib_edge[0].astype(F32)).astype(BF)
    d_nxt = (mine[5].astype(F32) + sib_edge[1].astype(F32)).astype(BF)
    sib_mid, d_prev, d_nxt = lax.optimization_barrier((sib_mid, d_prev, d_nxt))
    to_last = lax.ppermute(d_prev, LINE, BACK)
    to_first = lax.ppermute(d_nxt, LINE, FORTH)
    sib_mid = swapped(sib_mid)

    def terms(col, *at):
        return mine[col, *at].astype(F32) + sib_mid[col - 1, *at].astype(F32)

    d_side = [terms(time + 1, 2) for time in range(4)]
    d_side[0] += to_first[2].astype(F32)
    d_side[3] += to_last[2].astype(F32)
    to_inner = lax.ppermute(jnp.stack(d_side).astype(BF), Z, Z_PAIRS)
    is_inner = (jnp.arange(2) == 1 - zm)[:, None, None, None, None]
    d_own = []
    for time in range(4):
        total = terms(time + 1, slice(0, 2)) + jnp.where(is_inner, to_inner[time][None].astype(F32), 0.0)
        if time == 0:
            total = total + to_first[:2].astype(F32)
        if time == 3:
            total = total + to_last[:2].astype(F32)
        d_own.append(total.astype(BF))
    grads = jnp.concatenate([jnp.stack(d_own), dq[:, :, :, None]], axis=3).reshape(HEADS, 3, PIECE, HD)
    grad_keys, grad_values, grad_queries = gather(zm_arg, to_heads(grads))
    return grad_queries, grad_keys, grad_values


def solution(mesh):
    fine = Mesh(mesh.devices.reshape(SIZES), AXES)
    rows = P(AXES, None)
    return jax.shard_map(
        per_device,
        mesh=fine,
        in_specs=(rows, rows, rows, rows, P()),
        out_specs=(rows, rows, rows),
        check_vma=False,
    )
```

```python
import functools

import jax
import jax.numpy as jnp
from jax import lax
from jax.experimental import pallas as pl
from jax.experimental.pallas import tpu as pltpu
from jax.sharding import Mesh, PartitionSpec as P

HD = 128
HEADS = 16
PIECE = 96
HALF = 192
TILE = 384
BF = jnp.bfloat16
F32 = jnp.float32
AXES = ("yl", "x", "zh", "zm", "zl", "yhh", "yhl", "c")
SIZES = (2, 4, 2, 2, 2, 2, 2, 2)
GROUP = ("zh", "yhh", "zl", "yhl")
Z = ("zh", "zm", "zl")
Z_PAIRS = [(1, 2), (2, 1), (5, 6), (6, 5), (0, 7), (7, 0), (4, 3), (3, 4)]
LINE = ("yl", "x")
FORTH = [(i, i + 1) for i in range(7)]
BACK = [(i + 1, i) for i in range(7)]
SWAP = [(0, 1), (1, 0)]
NEG = float("-inf")


def head_of(chip, zm):
    zh, yhh, zl, yhl = (chip // 8) % 2, (chip // 4) % 2, (chip // 2) % 2, chip % 2
    return ((zh * 2 + zl + zm) % 4) * 4 + yhh * 2 + yhl


def spread_kernel(zm_ref, a_ref, b_ref, out_ref):
    zm = zm_ref[0]
    for chip in range(HEADS):
        columns = pl.ds(pl.multiple_of(head_of(chip, zm) * HD, HD), HD)
        out_ref[chip, 0] = a_ref[:, columns]
        out_ref[chip, 1] = b_ref[:, columns]


def spread(zm, a, b):
    return pl.pallas_call(
        spread_kernel,
        out_shape=jax.ShapeDtypeStruct((HEADS, 2, PIECE, HD), BF),
        in_specs=[pl.BlockSpec(memory_space=pltpu.SMEM)] + [pl.BlockSpec(memory_space=pltpu.VMEM)] * 2,
        out_specs=pl.BlockSpec(memory_space=pltpu.VMEM),
        cost_estimate=pl.CostEstimate(flops=0, bytes_accessed=4 * 393216, transcendentals=0),
    )(zm, a, b)


def gather_kernel(count, zm_ref, in_ref, *out_refs):
    zm = zm_ref[0]
    for chip in range(HEADS):
        columns = pl.ds(pl.multiple_of(head_of(chip, zm) * HD, HD), HD)
        for n in range(count):
            out_refs[n][:, columns] = in_ref[chip, n]


def gather(zm, blocks):
    count = blocks.shape[1]
    return pl.pallas_call(
        functools.partial(gather_kernel, count),
        out_shape=[jax.ShapeDtypeStruct((PIECE, HEADS * HD), BF)] * count,
        in_specs=[pl.BlockSpec(memory_space=pltpu.SMEM), pl.BlockSpec(memory_space=pltpu.VMEM)],
        out_specs=[pl.BlockSpec(memory_space=pltpu.VMEM)] * count,
        cost_estimate=pl.CostEstimate(flops=0, bytes_accessed=2 * count * 393216, transcendentals=0),
    )(zm, blocks)


def dot(a, b, dims):
    return lax.dot_general(a, b, (dims, ((), ())), preferred_element_type=F32)


def attention_kernel(
    zm_ref, chip_ref, line_ref, window_ref, own, own_s, side, side_s, prev, prev_s, nxt, nxt_s, qg,
    dq_out, mine_out, sib_edge, sib_mid,
    k_buf, v_buf, q_buf, g_buf, dk_acc, dv_acc, s_main, s_side, p_main, p_side, sems,
):
    zm, line = zm_ref[0], line_ref[0]
    head = head_of(chip_ref[0], zm)
    reach_t, reach_h = window_ref[head, 0], window_ref[head, 1]
    first_col = jnp.where(line == 0, 1, 0)
    last_col = jnp.where(line == 7, 4, 5)
    zls = (zm, 1 - zm)
    copies = []

    def copy(src, dst):
        c = pltpu.make_async_copy(src, dst, sems.at[len(copies)])
        c.start()
        copies.append(c)

    for kv, buf, part in ((0, k_buf, q_buf), (1, v_buf, g_buf)):
        copy(qg.at[:, :, :, kv], part)
        for core, (o, h, p, n) in enumerate(((own, side, prev, nxt), (own_s, side_s, prev_s, nxt_s))):
            copy(o.at[:, :, :, kv], buf.at[pl.ds(1, 4), pl.ds(0, 2), core])
            copy(h.at[:, :, kv], buf.at[pl.ds(1, 4), 2, core])
            copy(p.at[:, :, kv], buf.at[0, :, core])
            copy(n.at[:, :, kv], buf.at[5, :, core])
    for c in copies[: len(copies) // 2]:
        c.wait()

    scale2 = HD ** (-0.5) * 1.4426950408889634
    row_bias = jnp.where(reach_h >= 1, 0.0, NEG).astype(F32)

    def keys(buf, col):
        edge, inner, side = (buf[col, row].reshape(TILE, HD) for row in (*zls, 2))
        return jnp.concatenate([edge, inner], axis=0), side

    def queries(buf, time):
        return jnp.concatenate([buf[time, zl].reshape(HALF, HD) for zl in zls], axis=0)

    def lanes(j):
        return slice(j * 128, (j + 1) * 128)

    def finish(col, kv, block):
        block = (block * (1.0 if kv else HD ** (-0.5))).astype(BF).T
        for row in range(3):
            place = 2 if row == 2 else zls[row]
            sib, at = (sib_edge, col // 5) if col in (0, 5) else (sib_mid, col - 1)
            for core, out, at in ((0, mine_out, col), (1, sib, at)):
                for yhl in (0, 1):
                    start = row * TILE + core * HALF + yhl * PIECE
                    out[at, place, yhl, kv] = block[start : start + PIECE]

    def scores(time, d, slot, tops):
        col = time + d
        allowed = (col >= first_col) & (col <= last_col) & ((reach_t >= 1) | (d == 1))
        time_bias = jnp.where(allowed, 0.0, NEG).astype(F32)
        far_bias = time_bias + row_bias
        tops = list(tops)
        q = queries(q_buf, time)
        k01, k2 = keys(k_buf, col)
        s = dot(q, k01, ((1,), (1,))) * scale2
        for half in (0, 1):
            for j in range(6):
                part = s[half * HALF : (half + 1) * HALF, lanes(j)]
                if j // 3 != half:
                    part = part + far_bias
                elif d != 1:
                    part = part + time_bias
                s_main[slot, d, half * HALF : (half + 1) * HALF, lanes(j)] = part
                tops[half] = jnp.maximum(tops[half], part)
        s = dot(q[HALF:], k2, ((1,), (1,))) * scale2 + far_bias
        s_side[slot, d] = s
        for j in range(3):
            tops[1] = jnp.maximum(tops[1], s[:, lanes(j)])
        return tuple(tops)

    no_tops = (jnp.full((HALF, 128), NEG, F32),) * 2

    def one_time(time, slot, tops, after):
        q = queries(q_buf, time)
        g = queries(g_buf, time)
        g1 = g[HALF:]
        tops = [jnp.max(t, axis=1, keepdims=True) for t in tops]
        top = jnp.concatenate(tops, axis=0)
        total = jnp.zeros((TILE, 128), F32)
        delta = jnp.zeros((TILE, 128), F32)
        total1 = jnp.zeros((HALF, 128), F32)
        delta1 = jnp.zeros((HALF, 128), F32)
        for d in range(3):
            v01, v2 = keys(v_buf, time + d)
            p = dot(g, v01, ((1,), (1,)))
            p_main[d] = p
            for j in range(6):
                e = jnp.exp2(s_main[slot, d, :, lanes(j)] - top)
                s_main[slot, d, :, lanes(j)] = e
                total += e
                delta += e * p[:, lanes(j)]
            p = dot(g1, v2, ((1,), (1,)))
            p_side[d] = p
            for j in range(3):
                e = jnp.exp2(s_side[slot, d, :, lanes(j)] - tops[1])
                s_side[slot, d, :, lanes(j)] = e
                total1 += e
                delta1 += e * p[:, lanes(j)]
        total = jnp.concatenate([total[:HALF], total[HALF:] + total1], axis=0)
        delta = jnp.concatenate([delta[:HALF], delta[HALF:] + delta1], axis=0)
        inverse = 1.0 / jnp.sum(total, axis=1, keepdims=True)
        delta = jnp.sum(delta, axis=1, keepdims=True) * inverse
        qt, gt = q.T, g.T
        qt1, gt1 = qt[:, HALF:], gt[:, HALF:]
        dq = jnp.zeros((TILE, HD), F32)
        dq1 = jnp.zeros((HALF, HD), F32)
        next_tops = no_tops
        for d in range(3):
            col = time + d
            if after is not None:
                next_tops = scores(after, d, 1 - slot, next_tops)
            k01, k2 = keys(k_buf, col)
            w = s_main[slot, d] * inverse
            ds = (w * (p_main[d] - delta)).astype(BF)
            w1 = s_side[slot, d] * inverse[HALF:]
            ds1 = (w1 * (p_side[d] - delta[HALF:])).astype(BF)
            dq += dot(ds, k01, ((1,), (0,)))
            dq1 += dot(ds1, k2, ((1,), (0,)))
            main_k, last_k = dot(qt, ds, ((1,), (0,))), dot(qt1, ds1, ((1,), (0,)))
            main_v, last_v = dot(gt, w.astype(BF), ((1,), (0,))), dot(gt1, w1.astype(BF), ((1,), (0,)))
            for kv, acc, main, last in ((0, dk_acc, main_k, last_k), (1, dv_acc, main_v, last_v)):
                if d == 2 or (time == 0 and d == 1):
                    acc[col, :, 0 : 2 * TILE] = main
                    acc[col, :, 2 * TILE :] = last
                elif d == 1:
                    acc[col, :, 0 : 2 * TILE] += main
                    acc[col, :, 2 * TILE :] += last
                else:
                    block = jnp.concatenate([main, last], axis=1)
                    finish(col, kv, block if time == 0 else block + acc[col])
        dq = jnp.concatenate([dq[:HALF], dq[HALF:] + dq1], axis=0) * HD ** (-0.5)
        for row in (0, 1):
            dq_out[time, zls[row]] = dq[row * HALF : (row + 1) * HALF].astype(BF).reshape(2, PIECE, HD)
        return next_tops

    tops = no_tops
    for d in range(3):
        tops = scores(0, d, 0, tops)
    for c in copies[len(copies) // 2 :]:
        c.wait()

    for time in range(4):
        tops = one_time(time, time % 2, tops, time + 1 if time < 3 else None)
    for col in (4, 5):
        finish(col, 0, dk_acc[col])
        finish(col, 1, dv_acc[col])


def attention(*arrays):
    return pl.pallas_call(
        attention_kernel,
        out_shape=[
            jax.ShapeDtypeStruct((4, 2, 2, PIECE, HD), BF),
            jax.ShapeDtypeStruct((6, 3, 2, 2, PIECE, HD), BF),
            jax.ShapeDtypeStruct((2, 3, 2, 2, PIECE, HD), BF),
            jax.ShapeDtypeStruct((4, 3, 2, 2, PIECE, HD), BF),
        ],
        in_specs=[pl.BlockSpec(memory_space=pltpu.SMEM)] * 4 + [pl.BlockSpec(memory_space=pl.ANY)] * 9,
        out_specs=[pl.BlockSpec(memory_space=pltpu.VMEM)] * 4,
        scratch_shapes=[
            pltpu.VMEM((6, 3, 2, 2, PIECE, HD), BF),
            pltpu.VMEM((6, 3, 2, 2, PIECE, HD), BF),
            pltpu.VMEM((4, 2, 2, PIECE, HD), BF),
            pltpu.VMEM((4, 2, 2, PIECE, HD), BF),
            pltpu.VMEM((6, HD, 3 * TILE), F32),
            pltpu.VMEM((6, HD, 3 * TILE), F32),
            pltpu.VMEM((2, 3, TILE, 2 * TILE), F32),
            pltpu.VMEM((2, 3, HALF, TILE), F32),
            pltpu.VMEM((3, TILE, 2 * TILE), F32),
            pltpu.VMEM((3, HALF, TILE), F32),
            pltpu.SemaphoreType.DMA((18,)),
        ],
        compiler_params=pltpu.CompilerParams(vmem_limit_bytes=48 * 1024 * 1024),
        cost_estimate=pl.CostEstimate(flops=6 * 10**9, bytes_accessed=9 * 10**6, transcendentals=5 * 10**6),
    )(*arrays)


def to_heads(blocks):
    return lax.all_to_all(blocks, GROUP, split_axis=0, concat_axis=0, tiled=True)


def swapped(block):
    return lax.ppermute(block, "c", SWAP)


def scalar(value):
    return jnp.full((1,), value, jnp.int32)


def per_device(queries, keys, values, out_grad, window):
    at = {name: lax.axis_index(name) for name in AXES}
    zm = at["zm"]
    zm_arg = scalar(zm)
    line = scalar(at["yl"] * 4 + at["x"])
    chip = scalar(((at["zh"] * 2 + at["yhh"]) * 2 + at["zl"]) * 2 + at["yhl"])

    own = to_heads(spread(zm_arg, keys, values)).reshape(4, 2, 2, 2, PIECE, HD)
    inner = lax.dynamic_slice_in_dim(own, 1 - zm, 1, 1)[:, 0]
    qg = spread(zm_arg, queries, out_grad)
    side = lax.ppermute(inner, Z, Z_PAIRS)
    qg, side = lax.optimization_barrier((qg, side))
    qg = to_heads(qg).reshape(4, 2, 2, 2, PIECE, HD)
    own_s = swapped(own)
    nxt = lax.ppermute(jnp.concatenate([own[0], side[:1]], axis=0), LINE, BACK)
    prev = lax.ppermute(jnp.concatenate([own[3], side[3:]], axis=0), LINE, FORTH)
    dq, mine, sib_edge, sib_mid = attention(
        zm_arg, chip, line, window, own, own_s, side, swapped(side), prev, swapped(prev), nxt, swapped(nxt), qg
    )
    sib_edge = swapped(sib_edge)
    d_prev = (mine[0].astype(F32) + sib_edge[0].astype(F32)).astype(BF)
    d_nxt = (mine[5].astype(F32) + sib_edge[1].astype(F32)).astype(BF)
    sib_mid, d_prev, d_nxt = lax.optimization_barrier((sib_mid, d_prev, d_nxt))
    to_last = lax.ppermute(d_prev, LINE, BACK)
    to_first = lax.ppermute(d_nxt, LINE, FORTH)
    sib_mid = swapped(sib_mid)

    def terms(col, *at):
        return mine[col, *at].astype(F32) + sib_mid[col - 1, *at].astype(F32)

    to_mids = lax.ppermute(jnp.stack([terms(2, 2), terms(3, 2)]).astype(BF), Z, Z_PAIRS)
    to_mids, to_first, to_last = lax.optimization_barrier((to_mids, to_first, to_last))
    d_ends = [terms(1, 2) + to_first[2].astype(F32), terms(4, 2) + to_last[2].astype(F32)]
    to_ends = lax.ppermute(jnp.stack(d_ends).astype(BF), Z, Z_PAIRS)
    is_inner = (jnp.arange(2) == 1 - zm)[:, None, None, None, None]
    d_own = []
    for time in range(4):
        to_inner = to_mids[time - 1] if time in (1, 2) else to_ends[time // 3]
        total = terms(time + 1, slice(0, 2)) + jnp.where(is_inner, to_inner[None].astype(F32), 0.0)
        if time == 0:
            total = total + to_first[:2].astype(F32)
        if time == 3:
            total = total + to_last[:2].astype(F32)
        d_own.append(total.astype(BF))
    grads = jnp.concatenate([jnp.stack(d_own), dq[:, :, :, None]], axis=3).reshape(HEADS, 3, PIECE, HD)
    grad_keys, grad_values, grad_queries = gather(zm_arg, to_heads(grads))
    return grad_queries, grad_keys, grad_values


def solution(mesh):
    fine = Mesh(mesh.devices.reshape(SIZES), AXES)
    rows = P(AXES, None)
    return jax.shard_map(
        per_device,
        mesh=fine,
        in_specs=(rows, rows, rows, rows, P()),
        out_specs=(rows, rows, rows),
        check_vma=False,
    )
```

```python
import functools

import jax
import jax.numpy as jnp
from jax import lax
from jax.experimental import pallas as pl
from jax.experimental.pallas import tpu as pltpu
from jax.sharding import Mesh, PartitionSpec as P

HD = 128
HEADS = 16
PIECE = 96
HALF = 192
TILE = 384
BF = jnp.bfloat16
F32 = jnp.float32
AXES = ("yl", "x", "zh", "zm", "zl", "yhh", "yhl", "c")
SIZES = (2, 4, 2, 2, 2, 2, 2, 2)
GROUP = ("zh", "yhh", "zl", "yhl")
Z = ("zh", "zm", "zl")
Z_PAIRS = [(1, 2), (2, 1), (5, 6), (6, 5), (0, 7), (7, 0), (4, 3), (3, 4)]
LINE = ("yl", "x")
FORTH = [(i, i + 1) for i in range(7)]
BACK = [(i + 1, i) for i in range(7)]
SWAP = [(0, 1), (1, 0)]
NEG = float("-inf")


def head_of(chip, zm):
    zh, yhh, zl, yhl = (chip // 8) % 2, (chip // 4) % 2, (chip // 2) % 2, chip % 2
    return ((zh * 2 + zl + zm) % 4) * 4 + yhh * 2 + yhl


def spread_kernel(zm_ref, a_ref, b_ref, out_ref):
    zm = zm_ref[0]
    for chip in range(HEADS):
        columns = pl.ds(pl.multiple_of(head_of(chip, zm) * HD, HD), HD)
        out_ref[chip, 0] = a_ref[:, columns]
        out_ref[chip, 1] = b_ref[:, columns]


def spread(zm, a, b):
    return pl.pallas_call(
        spread_kernel,
        out_shape=jax.ShapeDtypeStruct((HEADS, 2, PIECE, HD), BF),
        in_specs=[pl.BlockSpec(memory_space=pltpu.SMEM)] + [pl.BlockSpec(memory_space=pltpu.VMEM)] * 2,
        out_specs=pl.BlockSpec(memory_space=pltpu.VMEM),
        cost_estimate=pl.CostEstimate(flops=0, bytes_accessed=4 * 393216, transcendentals=0),
    )(zm, a, b)


def gather_kernel(count, zm_ref, in_ref, *out_refs):
    zm = zm_ref[0]
    for chip in range(HEADS):
        columns = pl.ds(pl.multiple_of(head_of(chip, zm) * HD, HD), HD)
        for n in range(count):
            out_refs[n][:, columns] = in_ref[chip, n]


def gather(zm, blocks):
    count = blocks.shape[1]
    return pl.pallas_call(
        functools.partial(gather_kernel, count),
        out_shape=[jax.ShapeDtypeStruct((PIECE, HEADS * HD), BF)] * count,
        in_specs=[pl.BlockSpec(memory_space=pltpu.SMEM), pl.BlockSpec(memory_space=pltpu.VMEM)],
        out_specs=[pl.BlockSpec(memory_space=pltpu.VMEM)] * count,
        cost_estimate=pl.CostEstimate(flops=0, bytes_accessed=2 * count * 393216, transcendentals=0),
    )(zm, blocks)


def dot(a, b, dims):
    return lax.dot_general(a, b, (dims, ((), ())), preferred_element_type=F32)


def attention_kernel(
    zm_ref, chip_ref, line_ref, window_ref, own, own_s, side, side_s, prev, prev_s, nxt, nxt_s, qg,
    dq_out, mine_out, sib_edge, sib_mid,
    k_buf, v_buf, q_buf, g_buf, dk_acc, dv_acc, s_main, s_side, p_main, p_side, sems,
):
    zm, line = zm_ref[0], line_ref[0]
    head = head_of(chip_ref[0], zm)
    reach_t, reach_h = window_ref[head, 0], window_ref[head, 1]
    first_col = jnp.where(line == 0, 1, 0)
    last_col = jnp.where(line == 7, 4, 5)
    zls = (zm, 1 - zm)
    copies = []

    def copy(src, dst):
        c = pltpu.make_async_copy(src, dst, sems.at[len(copies)])
        c.start()
        copies.append(c)

    for kv, buf, part in ((0, k_buf, q_buf), (1, v_buf, g_buf)):
        copy(qg.at[:, :, :, kv], part)
        for core, (o, h, p, n) in enumerate(((own, side, prev, nxt), (own_s, side_s, prev_s, nxt_s))):
            copy(o.at[:, :, :, kv], buf.at[pl.ds(1, 4), pl.ds(0, 2), core])
            copy(h.at[:, :, kv], buf.at[pl.ds(1, 4), 2, core])
            copy(p.at[:, :, kv], buf.at[0, :, core])
            copy(n.at[:, :, kv], buf.at[5, :, core])
    for c in copies[: len(copies) // 2]:
        c.wait()

    scale2 = HD ** (-0.5) * 1.4426950408889634
    row_bias = jnp.where(reach_h >= 1, 0.0, NEG).astype(F32)

    def keys(buf, col):
        edge, inner, side = (buf[col, row].reshape(TILE, HD) for row in (*zls, 2))
        return jnp.concatenate([edge, inner], axis=0), side

    def queries(buf, time):
        return jnp.concatenate([buf[time, zl].reshape(HALF, HD) for zl in zls], axis=0)

    def lanes(j):
        return slice(j * 128, (j + 1) * 128)

    def finish(col, kv, block):
        block = (block * (1.0 if kv else HD ** (-0.5))).astype(BF).T
        for row in range(3):
            place = 2 if row == 2 else zls[row]
            sib, at = (sib_edge, col // 5) if col in (0, 5) else (sib_mid, col - 1)
            for core, out, at in ((0, mine_out, col), (1, sib, at)):
                for yhl in (0, 1):
                    start = row * TILE + core * HALF + yhl * PIECE
                    out[at, place, yhl, kv] = block[start : start + PIECE]

    def scores(time, d, slot, tops):
        col = time + d
        allowed = (col >= first_col) & (col <= last_col) & ((reach_t >= 1) | (d == 1))
        time_bias = jnp.where(allowed, 0.0, NEG).astype(F32)
        far_bias = time_bias + row_bias
        tops = list(tops)
        q = queries(q_buf, time)
        k01, k2 = keys(k_buf, col)
        s = dot(q, k01, ((1,), (1,))) * scale2
        for half in (0, 1):
            for j in range(6):
                part = s[half * HALF : (half + 1) * HALF, lanes(j)]
                if j // 3 != half:
                    part = part + far_bias
                elif d != 1:
                    part = part + time_bias
                s_main[slot, d, half * HALF : (half + 1) * HALF, lanes(j)] = part
                tops[half] = jnp.maximum(tops[half], part)
        s = dot(q[HALF:], k2, ((1,), (1,))) * scale2 + far_bias
        s_side[slot, d] = s
        for j in range(3):
            tops[1] = jnp.maximum(tops[1], s[:, lanes(j)])
        return tuple(tops)

    no_tops = (jnp.full((HALF, 128), NEG, F32),) * 2

    def one_time(time, slot, tops, after):
        q = queries(q_buf, time)
        g = queries(g_buf, time)
        g1 = g[HALF:]
        tops = [jnp.max(t, axis=1, keepdims=True) for t in tops]
        top = jnp.concatenate(tops, axis=0)
        total = jnp.zeros((TILE, 128), F32)
        delta = jnp.zeros((TILE, 128), F32)
        total1 = jnp.zeros((HALF, 128), F32)
        delta1 = jnp.zeros((HALF, 128), F32)
        for d in range(3):
            v01, v2 = keys(v_buf, time + d)
            p = dot(g, v01, ((1,), (1,)))
            p_main[d] = p
            for j in range(6):
                e = jnp.exp2(s_main[slot, d, :, lanes(j)] - top)
                s_main[slot, d, :, lanes(j)] = e
                total += e
                delta += e * p[:, lanes(j)]
            p = dot(g1, v2, ((1,), (1,)))
            p_side[d] = p
            for j in range(3):
                e = jnp.exp2(s_side[slot, d, :, lanes(j)] - tops[1])
                s_side[slot, d, :, lanes(j)] = e
                total1 += e
                delta1 += e * p[:, lanes(j)]
        total = jnp.concatenate([total[:HALF], total[HALF:] + total1], axis=0)
        delta = jnp.concatenate([delta[:HALF], delta[HALF:] + delta1], axis=0)
        inverse = 1.0 / jnp.sum(total, axis=1, keepdims=True)
        delta = jnp.sum(delta, axis=1, keepdims=True) * inverse
        qt, gt = q.T, g.T
        qt1, gt1 = qt[:, HALF:], gt[:, HALF:]
        dq = jnp.zeros((TILE, HD), F32)
        dq1 = jnp.zeros((HALF, HD), F32)
        next_tops = no_tops
        for d in range(3):
            col = time + d
            if after is not None:
                next_tops = scores(after, d, 1 - slot, next_tops)
            k01, k2 = keys(k_buf, col)
            w = s_main[slot, d] * inverse
            ds = (w * (p_main[d] - delta)).astype(BF)
            w1 = s_side[slot, d] * inverse[HALF:]
            ds1 = (w1 * (p_side[d] - delta[HALF:])).astype(BF)
            dq += dot(ds, k01, ((1,), (0,)))
            dq1 += dot(ds1, k2, ((1,), (0,)))
            main_k, last_k = dot(qt, ds, ((1,), (0,))), dot(qt1, ds1, ((1,), (0,)))
            main_v, last_v = dot(gt, w.astype(BF), ((1,), (0,))), dot(gt1, w1.astype(BF), ((1,), (0,)))
            for kv, acc, main, last in ((0, dk_acc, main_k, last_k), (1, dv_acc, main_v, last_v)):
                if d == 2 or (time == 0 and d == 1):
                    acc[col, :, 0 : 2 * TILE] = main
                    acc[col, :, 2 * TILE :] = last
                elif d == 1:
                    acc[col, :, 0 : 2 * TILE] += main
                    acc[col, :, 2 * TILE :] += last
                else:
                    block = jnp.concatenate([main, last], axis=1)
                    finish(col, kv, block if time == 0 else block + acc[col])
        dq = jnp.concatenate([dq[:HALF], dq[HALF:] + dq1], axis=0) * HD ** (-0.5)
        for row in (0, 1):
            dq_out[time, zls[row]] = dq[row * HALF : (row + 1) * HALF].astype(BF).reshape(2, PIECE, HD)
        return next_tops

    tops = no_tops
    for d in range(3):
        tops = scores(0, d, 0, tops)
    for c in copies[len(copies) // 2 :]:
        c.wait()

    for time in range(4):
        tops = one_time(time, time % 2, tops, time + 1 if time < 3 else None)
    for col in (4, 5):
        finish(col, 0, dk_acc[col])
        finish(col, 1, dv_acc[col])


def attention(*arrays):
    return pl.pallas_call(
        attention_kernel,
        out_shape=[
            jax.ShapeDtypeStruct((4, 2, 2, PIECE, HD), BF),
            jax.ShapeDtypeStruct((6, 3, 2, 2, PIECE, HD), BF),
            jax.ShapeDtypeStruct((2, 3, 2, 2, PIECE, HD), BF),
            jax.ShapeDtypeStruct((4, 3, 2, 2, PIECE, HD), BF),
        ],
        in_specs=[pl.BlockSpec(memory_space=pltpu.SMEM)] * 4 + [pl.BlockSpec(memory_space=pl.ANY)] * 9,
        out_specs=[pl.BlockSpec(memory_space=pltpu.VMEM)] * 4,
        scratch_shapes=[
            pltpu.VMEM((6, 3, 2, 2, PIECE, HD), BF),
            pltpu.VMEM((6, 3, 2, 2, PIECE, HD), BF),
            pltpu.VMEM((4, 2, 2, PIECE, HD), BF),
            pltpu.VMEM((4, 2, 2, PIECE, HD), BF),
            pltpu.VMEM((6, HD, 3 * TILE), F32),
            pltpu.VMEM((6, HD, 3 * TILE), F32),
            pltpu.VMEM((2, 3, TILE, 2 * TILE), F32),
            pltpu.VMEM((2, 3, HALF, TILE), F32),
            pltpu.VMEM((3, TILE, 2 * TILE), F32),
            pltpu.VMEM((3, HALF, TILE), F32),
            pltpu.SemaphoreType.DMA((18,)),
        ],
        compiler_params=pltpu.CompilerParams(vmem_limit_bytes=48 * 1024 * 1024),
        cost_estimate=pl.CostEstimate(flops=6 * 10**9, bytes_accessed=9 * 10**6, transcendentals=5 * 10**6),
    )(*arrays)


def to_heads(blocks):
    return lax.all_to_all(blocks, GROUP, split_axis=0, concat_axis=0, tiled=True)


def swapped(block):
    return lax.ppermute(block, "c", SWAP)


def scalar(value):
    return jnp.full((1,), value, jnp.int32)


def per_device(queries, keys, values, out_grad, window):
    at = {name: lax.axis_index(name) for name in AXES}
    zm = at["zm"]
    zm_arg = scalar(zm)
    line = scalar(at["yl"] * 4 + at["x"])
    chip = scalar(((at["zh"] * 2 + at["yhh"]) * 2 + at["zl"]) * 2 + at["yhl"])

    own = to_heads(spread(zm_arg, keys, values)).reshape(4, 2, 2, 2, PIECE, HD)
    inner = lax.dynamic_slice_in_dim(own, 1 - zm, 1, 1)[:, 0]
    qg = spread(zm_arg, queries, out_grad)
    side = lax.ppermute(inner, Z, Z_PAIRS)
    qg, side = lax.optimization_barrier((qg, side))
    qg = to_heads(qg).reshape(4, 2, 2, 2, PIECE, HD)
    own_s = swapped(own)
    nxt = lax.ppermute(jnp.concatenate([own[0], side[:1]], axis=0), LINE, BACK)
    prev = lax.ppermute(jnp.concatenate([own[3], side[3:]], axis=0), LINE, FORTH)
    dq, mine, sib_edge, sib_mid = attention(
        zm_arg, chip, line, window, own, own_s, side, swapped(side), prev, swapped(prev), nxt, swapped(nxt), qg
    )
    sib_edge = swapped(sib_edge)
    d_prev = (mine[0].astype(F32) + sib_edge[0].astype(F32)).astype(BF)
    d_nxt = (mine[5].astype(F32) + sib_edge[1].astype(F32)).astype(BF)
    to_last = lax.ppermute(d_prev, LINE, BACK)
    to_first = lax.ppermute(d_nxt, LINE, FORTH)
    sib_mid = swapped(sib_mid)

    def terms(col, *at):
        return mine[col, *at].astype(F32) + sib_mid[col - 1, *at].astype(F32)

    to_mids = lax.ppermute(jnp.stack([terms(2, 2), terms(3, 2)]).astype(BF), Z, Z_PAIRS)
    to_mids, to_first, to_last = lax.optimization_barrier((to_mids, to_first, to_last))
    d_ends = [terms(1, 2) + to_first[2].astype(F32), terms(4, 2) + to_last[2].astype(F32)]
    to_ends = lax.ppermute(jnp.stack(d_ends).astype(BF), Z, Z_PAIRS)
    is_inner = (jnp.arange(2) == 1 - zm)[:, None, None, None, None]
    d_own = []
    for time in range(4):
        to_inner = to_mids[time - 1] if time in (1, 2) else to_ends[time // 3]
        total = terms(time + 1, slice(0, 2)) + jnp.where(is_inner, to_inner[None].astype(F32), 0.0)
        if time == 0:
            total = total + to_first[:2].astype(F32)
        if time == 3:
            total = total + to_last[:2].astype(F32)
        d_own.append(total.astype(BF))
    grads = jnp.concatenate([jnp.stack(d_own), dq[:, :, :, None]], axis=3).reshape(HEADS, 3, PIECE, HD)
    grad_keys, grad_values, grad_queries = gather(zm_arg, to_heads(grads))
    return grad_queries, grad_keys, grad_values


def solution(mesh):
    fine = Mesh(mesh.devices.reshape(SIZES), AXES)
    rows = P(AXES, None)
    return jax.shard_map(
        per_device,
        mesh=fine,
        in_specs=(rows, rows, rows, rows, P()),
        out_specs=(rows, rows, rows),
        check_vma=False,
    )
```
